32 devices in a mesh: groups: 2 (over x), ex: 16 (over z, y, core).
Axes of the slice: x: 2, y: 2, z: 4, core: 2. Of those that a mesh axis runs over, the one named last changes fastest.
Arguments:
- tiles: bfloat16 [128, 32, 128, 128], P(('groups', 'ex')), parts along dimension 0, may hold values from -1.5 to 1.5
- column_blocks: int32 [128, 32], P(('groups', 'ex')), parts along dimension 0, may hold values from 0 to 8191
- occupied: int32 [128, 32], P(('groups', 'ex')), parts along dimension 0, may hold values 0 or 1
- labels: int32 [128, 128], P(('groups', 'ex')), parts along dimension 0, may hold values from -1 to 1, as said below
- weights: float32 [16384, 128], P(('groups', 'ex')), parts along dimension 0, may hold values from -0.6 to 0.6
Outputs:
- newton_step: float32 [16384, 128], P(('groups', 'ex')), parts along dimension 0
- residual: float32 [16384, 128], P(('groups', 'ex')), parts along dimension 0
The draws below stay inside these ranges and needn't reach their ends.
There are 2 independent parts, one for each index of `groups`. The reference program is written for one: setup_inputs(seed, part) draws one part's arguments, and reference() takes and returns one part's arrays. A program takes and returns all parts, laid end to end along the dimension named above; each array names one. Nothing has to cross between parts.
Inputs may be any that keep to these rules, and one draw needn't show every extreme that they name: `labels`: each label is -1 or +1, never 0.
All inputs are finite; a program needn't handle non-finite values. No bound on the sum of `occupied` on one device may be relied on, other than what follows from the above.
Results may differ from the reference program's by a relative error of at most 0.012.
The reference program's roundings to bfloat16 on the way count: a program that leaves them out, or rounds other values in their place, can miss the bound.
Values may be sent and summed in bfloat16 or wider, within the bound.
No kernel may reach another device: no remote copies, remote signals or barrier semaphores. Data moves between devices by JAX's collectives and lax.ppermute only.
A program may use at most 64 MiB of HBM per device.

```python
import jax
import jax.numpy as jnp

TILE = 128
FB = 8192
K = 32
ITERS = 3
ROWBLK = 64


def draw_labels(key, part):
    key = jax.random.fold_in(key, 7)
    coins = jax.random.randint(key, (ROWBLK, TILE), 0, 2)
    return (2 * coins - 1).astype(jnp.int32)


def plant(result, stream_key, low, top_value):
    dims = result.shape
    place = [jax.random.randint(jax.random.fold_in(stream_key, axis), (), 0, dims[axis]) for axis in range(len(dims))]
    result = result.at[tuple(place)].set(low)
    longest = dims.index(max(dims))
    place[longest] = (place[longest] + 1) % dims[longest]
    return result.at[tuple(place)].set(top_value)


def steps_of(stream_key, extent, pieces, least, high):
    def one(axis_at, parts):
        steps = jax.random.uniform(jax.random.fold_in(jax.random.fold_in(stream_key, 6), axis_at), (parts,), jnp.float32, least / len(pieces), high / len(pieces))
        return jnp.repeat(jnp.exp(steps), extent[axis_at] // parts).reshape((-1,) + (1,) * (len(extent) - axis_at - 1))

    factor_of = one(*pieces[0])
    for cut in pieces[1:]:
        factor_of = factor_of * one(*cut)
    return factor_of


def noise(rng, dims, width, most, pieces=(), dtype=jnp.bfloat16):
    factor_of = steps_of(rng, dims, pieces, -0.22, 0.18) if pieces else 1.0
    values = jax.random.normal(rng, dims, jnp.float32) * width * factor_of
    return jnp.minimum(jnp.maximum(values, -most), most).astype(dtype)


def setup_inputs(seed: int = 0, part: int = 0) -> dict:
    splits = jax.random.split(jax.random.key(seed), 6)
    part_splits = jax.random.split(jax.random.fold_in(splits[5], part), 6)
    return {
        "tiles": noise(part_splits[0], (ROWBLK, K, TILE, TILE), 0.25, 1.5, ((0, 16),)),
        "column_blocks": plant(jax.random.randint(part_splits[1], (ROWBLK, K), 0, FB), jax.random.fold_in(part_splits[1], 1), 0, FB - 1).astype(jnp.int32),
        "occupied": plant((jax.random.randint(part_splits[2], (ROWBLK, K), 0, 4) < 3).astype(jnp.int32), jax.random.fold_in(part_splits[2], 1), 0, 1),
        "labels": draw_labels(jax.random.fold_in(jax.random.fold_in(splits[5], part), 71), part),
        "weights": noise(part_splits[4], (FB, TILE), 0.1, 0.6, ((0, 16),), jnp.float32),
    }


ridge = 1.0


def apply_rows(tiles, column_blocks, occupancy, vector):
    picked = vector[column_blocks] * occupancy[:, :, None]
    return jnp.einsum("bkij,bkj->bi", tiles.astype(jnp.float32), picked.astype(jnp.float32))


def apply_columns(tiles, column_blocks, occupancy, values):
    contrib = jnp.einsum("bkij,bi->bkj", tiles.astype(jnp.float32), values.astype(jnp.float32))
    contrib = contrib * occupancy[:, :, None].astype(jnp.float32)
    return jax.ops.segment_sum(contrib.reshape(-1, TILE), column_blocks.reshape(-1), num_segments=FB)


def reference(tiles, column_blocks, occupied, labels, weights):
    occupancy = occupied.astype(jnp.bfloat16)
    signs = labels.astype(jnp.float32)
    margins = apply_rows(tiles, column_blocks, occupancy, weights.astype(jnp.bfloat16))
    prob = jax.nn.sigmoid(-signs * margins)
    curv = prob * (1.0 - prob)
    slopes = (-signs * prob).astype(jnp.bfloat16)
    gradient = apply_columns(tiles, column_blocks, occupancy, slopes) + ridge * weights
    squares = (tiles.astype(jnp.float32) * tiles.astype(jnp.float32)).astype(jnp.bfloat16)
    precond = apply_columns(squares, column_blocks, occupancy, curv.astype(jnp.bfloat16)) + ridge
    newton_step = jnp.zeros_like(weights)
    residual = -gradient
    scaled = residual / precond
    direction = scaled
    res_dot = jnp.sum(residual * scaled)
    for step in range(ITERS):
        moved = apply_rows(tiles, column_blocks, occupancy, direction.astype(jnp.bfloat16))
        image = apply_columns(tiles, column_blocks, occupancy, (curv * moved).astype(jnp.bfloat16)) + ridge * direction
        alpha = res_dot / jnp.sum(direction * image)
        newton_step = newton_step + alpha * direction
        residual = residual - alpha * image
        scaled = residual / precond
        next_dot = jnp.sum(residual * scaled)
        direction = scaled + (next_dot / res_dot) * direction
        res_dot = next_dot
    return newton_step, residual
```

```python
import functools

import jax
import jax.numpy as jnp
from jax import lax
from jax.experimental import pallas as pl
from jax.experimental.pallas import tpu as pltpu
from jax.sharding import PartitionSpec as P

RIDGE = 1.0
TAIL = 16
DIGIT = 128.0
F32 = jnp.float32
BF16 = jnp.bfloat16
VMEM = pl.BlockSpec(memory_space=pltpu.VMEM)
ANY = pl.BlockSpec(memory_space=pl.ANY)


def iota(shape, axis):
    return lax.broadcasted_iota(jnp.int32, shape, axis)


def params():
    return pltpu.CompilerParams(vmem_limit_bytes=40 * 1024 * 1024)


def swap(x, first, second=None):
    n = lax.axis_size("ex")
    second = first if second is None else second
    return lax.ppermute(x, "ex", [(i, i ^ (second if i % 2 else first)) for i in range(n)])


def gather_blocks(x):
    n = lax.axis_size("ex")
    pair = jnp.concatenate([x, swap(x, 1)], axis=0)
    chips = list(range(2, n, 2))
    blocks = [pair]
    split = [swap(pair, a, b) for a, b in zip(chips[0:-1:2], chips[1::2])]
    if len(chips) % 2:
        blocks.append(swap(pair, chips[-1]))
    for got in split:
        blocks += [got, swap(got, 1)]
    return blocks


def gather_wide(x):
    n = lax.axis_size("ex")
    across = [(s, swap(x, s)) for s in range(4, n, 4)]
    blocks = [(0, x), (2, swap(x, 2))] + across + [(s ^ 2, swap(got, 2)) for s, got in across]
    return blocks + [(s ^ 1, swap(got, 1)) for s, got in blocks]


def rounded(x):
    return x.astype(BF16).astype(F32)


def ids_of(tail):
    tail = tail.astype(F32)
    return tail[0:1] * DIGIT + tail[1:2]


def pieces(x):
    high = rounded(x)
    mid = rounded(x - high)
    return high, mid, x - high - mid


def tail_with(idtail, scalars):
    lanes = iota((1, idtail.shape[1]), 1)
    row = jnp.zeros((1, idtail.shape[1]), F32)
    for at, value in enumerate(scalars):
        row = jnp.where(lanes == at, value, row)
    out, rows = idtail, iota(idtail.shape, 0)
    for at, piece in enumerate(pieces(row)):
        out = jnp.where(rows == 2 + at, piece, out)
    return out.astype(BF16)


def total(x):
    return jnp.sum(jnp.sum(x, axis=0, keepdims=True), axis=1, keepdims=True)


def lane(row, at):
    return jnp.sum(jnp.where(iota(row.shape, 1) == at, row, 0.0), axis=1, keepdims=True)


def start_tiles(tiles_hbm, tiles, sems):
    copies = [pltpu.make_async_copy(tiles_hbm.at[b], tiles.at[b], sems.at[b]) for b in range(tiles.shape[0])]
    for copy in copies:
        copy.start()
    return copies


def rows_times(tiles, b, vec):
    k_all = tiles.shape[1]

    def body(k, acc):
        return acc + tiles[b, k].astype(F32) * vec[pl.ds(b * k_all + k, 1), :]

    acc = lax.fori_loop(0, k_all, body, jnp.zeros(tiles.shape[2:], F32), unroll=8)
    return jnp.sum(acc, axis=1, keepdims=True)


def columns_times(tiles, b, u, out):
    k_all = tiles.shape[1]

    def body(k, carry):
        out[pl.ds(b * k_all + k, 1), :] = jnp.sum(tiles[b, k].astype(F32) * u, axis=0, keepdims=True)
        return carry

    lax.fori_loop(0, k_all, body, 0, unroll=8)


def prep_kernel(cols_ref, occ_ref, w_ref, payload_ref, ccol_ref, idtail_ref):
    per, width = w_ref.shape
    payload_ref[0:per, :] = w_ref[...].astype(BF16)
    ids = jnp.where(occ_ref[...] > 0, cols_ref[...], -1).astype(F32)
    rows, k_all = ids.shape
    row = jnp.concatenate([ids[r : r + 1] for r in range(rows)], axis=1)
    high = jnp.floor(row * (1.0 / DIGIT))
    low = row - high * DIGIT
    at = iota((TAIL, width), 0)
    tail = jnp.where(at == 0, high, jnp.where(at == 1, low, 0.0))
    idtail_ref[...] = tail
    payload_ref[per : per + TAIL, :] = tail.astype(BF16)
    ccol_ref[...] = jnp.transpose(jnp.broadcast_to(row, (width, width)))


def first_kernel(xors, me_ref, *refs):
    n = len(xors)
    blocks = refs[:n]
    ccol_ref, idtail_ref, labels_ref, tiles_hbm = refs[n : n + 4]
    payload_ref, wslot_ref, curv_ref, grad_ref = refs[n + 4 : n + 8]
    tiles, tg, td, sems = refs[n + 8 :]
    copies = start_tiles(tiles_hbm, tiles, sems)
    slots, width = ccol_ref.shape
    per = blocks[0].shape[0] - TAIL
    r_all, k_all = tiles.shape[:2]
    me = me_ref[0]
    ccol = ccol_ref[...]
    occupied = ccol >= 0.0
    acc = jnp.zeros((slots, width), F32)
    for xor, block in zip(xors, blocks):
        base = ((me ^ xor) * per).astype(F32)
        at = ccol - base
        hot = jnp.concatenate(
            [(at == (iota((slots, width), 1) + q * width).astype(F32)).astype(F32).astype(BF16) for q in range(per // width)],
            axis=1,
        )
        acc = acc + jnp.dot(hot, block[0:per, :], preferred_element_type=F32)
    wslot_ref[...] = acc
    for b in range(r_all):
        copies[b].wait()
        margin = rows_times(tiles, b, wslot_ref)
        sign = jnp.transpose(jnp.broadcast_to(labels_ref[b : b + 1, :].astype(F32), (width, width)))
        prob = jax.nn.sigmoid(-sign * margin)
        curv = prob * (1.0 - prob)
        curv_ref[b] = curv
        slope = rounded(-sign * prob)
        weight = rounded(curv)

        def body(k, carry):
            x = tiles[b, k]
            tg[pl.ds(b * k_all + k, 1), :] = jnp.sum(x.astype(F32) * slope, axis=0, keepdims=True)
            td[pl.ds(b * k_all + k, 1), :] = jnp.sum((x * x).astype(F32) * weight, axis=0, keepdims=True)
            return carry

        lax.fori_loop(0, k_all, body, 0, unroll=4)
    grad = jnp.where(occupied, tg[...], 0.0)
    grad_ref[...] = grad
    payload_ref[0:slots, :] = grad.astype(BF16)
    payload_ref[slots : 2 * slots, :] = jnp.where(occupied, td[...], 0.0).astype(BF16)
    payload_ref[2 * slots : 2 * slots + TAIL, :] = idtail_ref[...].astype(BF16)


def apply_and_pack(copies, tiles, ccol, z, zrows, terms, curv_ref, weight, more, payload_ref, terms_ref, idtail_ref, res):
    slots = ccol.shape[0]
    zrows[...] = z
    quad = jnp.zeros((1, 1), F32)
    for b in range(tiles.shape[0]):
        if copies is not None:
            copies[b].wait()
        moved = rows_times(tiles, b, zrows)
        u = curv_ref[b] * moved
        quad = quad + jnp.sum(u[:, 0:1] * moved, axis=0, keepdims=True)
        columns_times(tiles, b, u, terms)
    found = jnp.where(ccol >= 0.0, terms[...], 0.0)
    terms_ref[...] = found
    payload_ref[0:slots, :] = found.astype(BF16)
    at = payload_ref.shape[0] - TAIL
    scalars = [total(weight * res * z), total(weight * z * z) + quad] + more
    payload_ref[at : at + TAIL, :] = tail_with(idtail_ref[...], scalars)


def hot_of(ccol, block, at):
    return (ccol == ids_of(block[at : at + TAIL, :])).astype(F32)


def start_kernel(n, *refs):
    blocks = refs[:n]
    ccol_ref, idtail_ref, wslot_ref, curv_ref, part_ref, tiles_hbm = refs[n : n + 6]
    payload_ref, m_ref, r_ref, z_ref, weight_ref, terms_ref = refs[n + 6 : n + 12]
    tiles, zrows, terms, sems = refs[n + 12 :]
    copies = start_tiles(tiles_hbm, tiles, sems)
    ccol = ccol_ref[...]
    slots, width = ccol.shape
    each = 2 * slots + TAIL
    acc = jnp.zeros((slots, 2 * width), F32)
    count = jnp.zeros((slots, width), F32)
    for block in blocks:
        for at in range(0, block.shape[0], each):
            hot = hot_of(ccol, block, at + 2 * slots)
            count = count + hot
            both = jnp.concatenate([block[at : at + slots, :], block[at + slots : at + 2 * slots, :]], axis=1)
            acc = acc + jnp.dot(hot.astype(BF16), both, preferred_element_type=F32)
    weight = 1.0 / jnp.sum(count, axis=1, keepdims=True)
    weight_ref[...] = jnp.broadcast_to(weight, (slots, width))
    m = acc[:, width:] + RIDGE
    r = -(acc[:, :width] + RIDGE * wslot_ref[...])
    z = r / m
    m_ref[...] = m
    r_ref[...] = r
    z_ref[...] = z
    apply_and_pack(
        copies, tiles, ccol, z, zrows, terms, curv_ref, weight, [jnp.zeros((1, 1), F32), part_ref[0:1, 0:1]],
        payload_ref, terms_ref, idtail_ref, r,
    )


def untouched_kernel(xors, me_ref, w_ref, *refs):
    tails, out_ref = refs[:-1], refs[-1]
    per, width = w_ref.shape
    mine = (iota((per, width), 0) + me_ref[0] * per).astype(F32)
    count = jnp.zeros((per, width), F32)
    for tail in tails:
        count = count + (mine == ids_of(tail[per : per + TAIL, :])).astype(F32)
    free = jnp.sum(count, axis=1, keepdims=True) == 0.0
    w = w_ref[...]
    out_ref[...] = jnp.broadcast_to(total(jnp.where(free, w * w, 0.0)), out_ref.shape)


def sums_of(blocks):
    row = None
    for block in blocks:
        each = block.shape[0] // 2
        for at in (each, 2 * each):
            tail = block[at - TAIL : at, :].astype(F32)
            part = tail[2:3] + tail[3:4] + tail[4:5]
            row = part if row is None else row + part
    return row


def step_scalars(first, row, state):
    delta, zaz, zs = lane(row, 0), lane(row, 1), lane(row, 2)
    if first:
        free = lane(row, 3)
        rho = sigma = jnp.ones((1, 1), F32)
        delta, zaz = delta + free, zaz + free
        beta = jnp.zeros((1, 1), F32)
        pap = zaz
    else:
        delta_old, pap_old, rho, sigma, free = (lane(state, at) for at in range(5))
        delta, zaz, zs = delta + rho * rho * free, zaz + rho * rho * free, zs + rho * sigma * free
        beta = delta / delta_old
        pap = zaz + 2.0 * beta * zs + beta * beta * pap_old
        sigma = rho + beta * sigma
    alpha = delta / pap
    rho = rho - alpha * sigma
    return delta, pap, rho, sigma, free, alpha, beta


def pack_row(scalars, shape):
    out = jnp.zeros(shape, F32)
    for at, value in enumerate(scalars):
        out = jnp.where(iota(shape, 1) == at, value, out)
    return out


def step_kernel(first, n, *refs):
    blocks = refs[:n]
    ccol_ref, idtail_ref, curv_ref, weight_ref, m_ref, r_in, z_in, s_in, state_in = refs[n : n + 9]
    terms_in, sent_in, owed_in, tiles_hbm = refs[n + 9 : n + 13]
    payload_ref, r_ref, z_ref, s_ref, state_ref, terms_ref, sent_ref, owed_ref = refs[n + 13 : n + 21]
    tiles, zrows, terms, sems = refs[n + 21 :]
    copies = start_tiles(tiles_hbm, tiles, sems)
    ccol = ccol_ref[...]
    slots, width = ccol.shape
    each = slots + TAIL
    scalars = step_scalars(first, sums_of(blocks), state_in[0:1, :])
    alpha, beta = scalars[5:7]
    state_ref[...] = pack_row(scalars, state_ref.shape)
    image = z_in[...]
    for block in blocks:
        for at in range(0, block.shape[0], each):
            hot = hot_of(ccol, block, at + slots).astype(BF16)
            image = image + jnp.dot(hot, block[at : at + slots, :], preferred_element_type=F32)
    s = image if first else image + beta * s_in[...]
    r = r_in[...] - alpha * s
    z = r / m_ref[...]
    s_ref[...] = s
    r_ref[...] = r
    z_ref[...] = z
    sent = terms_in[...] if first else terms_in[...] + beta * sent_in[...]
    owed = owed_in[...] + alpha * sent
    sent_ref[...] = sent
    owed_ref[...] = owed
    if payload_ref.shape[0] > each:
        payload_ref[slots : 2 * slots, :] = owed.astype(BF16)
    weight = weight_ref[...]
    apply_and_pack(
        copies, tiles, ccol, z, zrows, terms, curv_ref, weight, [total(weight * z * s)], payload_ref, terms_ref,
        idtail_ref, r,
    )


def last_kernel(n, iters, me_ref, w_ref, state_a, state_b, *refs):
    lists = [refs[i * n : (i + 1) * n] for i in range(iters + 1)]
    newton_ref, residual_ref, stack, hots = refs[(iters + 1) * n :]
    per, width = w_ref.shape
    first_each = lists[0][0].shape[0] // 2
    slots = (first_each - TAIL) // 2
    mine = (iota((per, width), 0) + me_ref[0] * per).astype(F32)
    row = 0
    for index in range(n):
        for half in range(2):
            at = half * first_each
            block = lists[0][index]
            hots[:, row : row + slots] = hot_of(mine, block, at + 2 * slots).astype(BF16)
            stack[row : row + slots, 0:width] = block[at : at + slots, :]
            stack[row : row + slots, width : 2 * width] = block[at + slots : at + 2 * slots, :]
            for it in range(iters):
                low = half * (lists[1 + it][index].shape[0] // 2)
                stack[row : row + slots, (2 + it) * width : (3 + it) * width] = lists[1 + it][index][low : low + slots, :]
            stack[row : row + slots, (2 + iters) * width :] = lists[iters][index][low + slots : low + 2 * slots, :]
            row += slots
    state_c = pack_row(step_scalars(False, sums_of(lists[iters]), state_b[0:1, :]), (1, width))
    states = [state_a[0:1, :], state_b[0:1, :], state_c]
    for low in range(0, per, width):
        sums = jnp.dot(hots[low : low + width, :], stack[...], preferred_element_type=F32)
        g, d = sums[:, 0:width], sums[:, width : 2 * width]
        w = w_ref[low : low + width, :]
        m = d + RIDGE
        r = -(g + RIDGE * w)
        x = jnp.zeros_like(r)
        p = s = None
        for it in range(iters):
            alpha, beta = lane(states[it], 5), lane(states[it], 6)
            z = r / m
            image = sums[:, (2 + it) * width : (3 + it) * width] + RIDGE * z
            p = z if it == 0 else z + beta * p
            s = image if it == 0 else image + beta * s
            if it == iters - 1:
                r = -(sums[:, (2 + iters) * width :] + RIDGE * w) - RIDGE * x
            x = x + alpha * p
            r = r - alpha * s
        newton_ref[low : low + width, :] = x
        residual_ref[low : low + width, :] = r


def local(tiles, column_blocks, occupied, labels, weights):
    me = lax.axis_index("ex").astype(jnp.int32).reshape(1)
    per, width = weights.shape
    r_all, k_all = tiles.shape[:2]
    slots = r_all * k_all
    n_dev = lax.axis_size("ex")
    smem = pl.BlockSpec(memory_space=pltpu.SMEM)
    sds = jax.ShapeDtypeStruct
    square = sds((slots, width), F32)

    payload, ccol, idtail = pl.pallas_call(
        prep_kernel,
        out_shape=(sds((per + TAIL, width), BF16), square, sds((TAIL, width), F32)),
        in_specs=[VMEM] * 3,
        out_specs=(VMEM,) * 3,
        compiler_params=params(),
        name="prep",
    )(column_blocks, occupied, weights)

    wide = gather_wide(payload)
    xors, wide = [xor for xor, _ in wide], [block for _, block in wide]
    tile_scratch = pltpu.VMEM(tiles.shape, BF16)
    sems = pltpu.SemaphoreType.DMA((r_all,))
    cell = pltpu.VMEM((slots, width), F32)

    payload, wslot, curv, grad = pl.pallas_call(
        functools.partial(first_kernel, xors),
        out_shape=(sds((2 * slots + TAIL, width), BF16), square, sds((r_all, width, width), F32), square),
        in_specs=[smem] + [VMEM] * (len(wide) + 3) + [ANY],
        out_specs=(VMEM,) * 4,
        scratch_shapes=[tile_scratch, cell, cell, sems],
        compiler_params=params(),
        name="margins",
    )(me, *wide, ccol, idtail, labels, tiles)

    part = pl.pallas_call(
        functools.partial(untouched_kernel, xors),
        out_shape=sds((8, width), F32),
        in_specs=[smem] + [VMEM] * (len(wide) + 1),
        out_specs=VMEM,
        compiler_params=params(),
        name="untouched",
    )(me, weights, *wide)

    exchanged = [gather_blocks(payload)]
    n = len(exchanged[0])
    payload_shape = sds((slots + TAIL, width), BF16)
    scratch = [tile_scratch, cell, cell, sems]
    payload, m, r, z, weight, terms = pl.pallas_call(
        functools.partial(start_kernel, n),
        out_shape=(payload_shape, square, square, square, square, square),
        in_specs=[VMEM] * (n + 5) + [ANY],
        out_specs=(VMEM,) * 6,
        scratch_shapes=scratch,
        compiler_params=params(),
        name="start",
    )(*exchanged[0], ccol, idtail, wslot, curv, part, tiles)

    iters = 3
    states, s, state, sent, owed = [], z, part, terms, grad
    for it in range(iters - 1):
        exchanged.append(gather_blocks(payload))
        shape = payload_shape if it < iters - 2 else sds((2 * slots + TAIL, width), BF16)
        payload, r, z, s, state, terms, sent, owed = pl.pallas_call(
            functools.partial(step_kernel, it == 0, n),
            out_shape=(shape, square, square, square, sds((8, width), F32), square, square, square),
            in_specs=[VMEM] * (n + 12) + [ANY],
            out_specs=(VMEM,) * 8,
            scratch_shapes=scratch,
            compiler_params=params(),
            name=f"step_{it}",
        )(*exchanged[-1], ccol, idtail, curv, weight, m, r, z, s, state, terms, sent, owed, tiles)
        states.append(state)
    exchanged.append(gather_blocks(payload))

    flat = [block for blocks in exchanged for block in blocks]
    return pl.pallas_call(
        functools.partial(last_kernel, n, iters),
        out_shape=(sds(weights.shape, F32), sds(weights.shape, F32)),
        in_specs=[smem] + [VMEM] * (3 + len(flat)),
        out_specs=(VMEM, VMEM),
        scratch_shapes=[
            pltpu.VMEM((n_dev * slots, (3 + iters) * width), BF16),
            pltpu.VMEM((per, n_dev * slots), BF16),
        ],
        compiler_params=params(),
        name="finish",
    )(me, weights, *states, *flat)


def solution(mesh):
    placed = (
        P(("groups", "ex"), None, None, None),
        P(("groups", "ex"), None),
        P(("groups", "ex"), None),
        P(("groups", "ex"), None),
        P(("groups", "ex"), None),
    )
    return jax.shard_map(
        local,
        mesh=mesh,
        in_specs=placed,
        out_specs=(P(("groups", "ex"), None), P(("groups", "ex"), None)),
        check_vma=False,
    )
```
